32 devices in a mesh: wide: 16 (over z, x, core), narrow: 2 (over y).
Axes of the slice: x: 2, y: 2, z: 4, core: 2. Of those that a mesh axis runs over, the one named last changes fastest.
Arguments:
- video_q: bfloat16 [36864, 3072], P(('wide', 'narrow')), may hold values from -8 to 8
- video_k: bfloat16 [36864, 3072], P(('wide', 'narrow')), may hold values from -6 to 6
- video_v: bfloat16 [36864, 3072], P(('wide', 'narrow')), may hold values from -6 to 6
- text_q: bfloat16 [256, 3072], P(None, 'narrow'), may hold values from -8 to 8
- text_k: bfloat16 [256, 3072], P(None, 'narrow'), may hold values from -6 to 6
- text_v: bfloat16 [256, 3072], P(None, 'narrow'), may hold values from -6 to 6
- text_len: int32 [1], replicated, may hold values from 128 to 256
- win_start: int32 [96], replicated, may hold values from 0 to 1, as said below
Outputs:
- video_out: bfloat16 [36864, 3072], P(('wide', 'narrow'))
- text_out: bfloat16 [256, 3072], P(None, 'narrow')
The draws below stay inside these ranges and needn't reach their ends.
Inputs may be any that keep to these rules, and one draw needn't show every extreme that they name: `win_start`: the window of 2 tile columns always holds the tile's own column.
All inputs are finite; a program needn't handle non-finite values.
Results may differ from the reference program's by a relative error of at most 0.0039.
Values may be sent and summed in bfloat16 or wider, within the bound.
No kernel may reach another device: no remote copies, remote signals or barrier semaphores. Data moves between devices by JAX's collectives and lax.ppermute only.
A program may use at most 384 MiB of HBM per device.

```python
import jax
import jax.numpy as jnp
from jax import lax

HEADS = 24
HDIM = 128
D = 3072
TT = 6
TH = 8
TW = 8
GH = 2
GW = 3
KT = 3
KW = 2
TXT = 256
TOKENS = 36864
NUM_TILES = 96
N_WIDE = 16


def shared_pieces(key, rows, salt):
    key = jax.random.fold_in(key, salt)
    parts = jax.random.split(key, 2)
    normal_q = jax.random.normal(parts[0], (rows, D), jnp.float32)
    normal_k = jax.random.normal(parts[1], (rows, D), jnp.float32)
    return (normal_q, normal_k)


def draw_video_q(key, part):
    normal_q, normal_k = shared_pieces(key, TOKENS, 11)
    return jnp.clip(2.5 * normal_q, -8.0, 8.0).astype(jnp.bfloat16)


def draw_video_k(key, part):
    normal_q, normal_k = shared_pieces(key, TOKENS, 11)
    return jnp.clip(normal_k, -6.0, 6.0).astype(jnp.bfloat16)


def draw_text_q(key, part):
    normal_q, normal_k = shared_pieces(key, TXT, 12)
    return jnp.clip(2.5 * normal_q, -8.0, 8.0).astype(jnp.bfloat16)


def draw_text_k(key, part):
    normal_q, normal_k = shared_pieces(key, TXT, 12)
    return jnp.clip(normal_k, -6.0, 6.0).astype(jnp.bfloat16)


def draw_win_start(key, part):
    key = jax.random.fold_in(key, 5)
    tiles = jnp.arange(NUM_TILES)
    column = tiles % GW
    lowest = jnp.maximum(0, column - KW + 1)
    highest = jnp.minimum(column, GW - KW)
    return (lowest + jax.random.randint(key, (NUM_TILES,), 0, highest - lowest + 1)).astype(jnp.int32)


def block_levels(stream_key, shape, cuts, low, largest):
    gain = 1.0
    for axis_at, blocks in cuts:
        draws = jax.random.uniform(jax.random.fold_in(jax.random.fold_in(stream_key, 6), axis_at), (blocks,), jnp.float32, low / len(cuts), largest / len(cuts))
        gain = gain * jnp.repeat(jnp.exp(draws), shape[axis_at] // blocks).reshape((-1,) + (1,) * (len(shape) - 1 - axis_at))
    return gain


def gaussian(stream_key, extent, scale, most, shards=(), kind=jnp.bfloat16):
    drawn = jax.random.normal(stream_key, extent, jnp.float32) * scale
    if len(shards) > 0:
        drawn = block_levels(stream_key, extent, shards, -0.22, 0.18) * drawn
    return jnp.clip(drawn, min=-most, max=most).astype(kind)


def setup_inputs(seed: int = 0) -> dict:
    splits = jax.random.split(jax.random.key(seed), 9)
    return {
        "video_q": draw_video_q(jax.random.fold_in(splits[8], 71), 0),
        "video_k": draw_video_k(jax.random.fold_in(splits[8], 71), 0),
        "video_v": gaussian(splits[2], (TOKENS, D), 1.0, 6.0, ((0, 32),)),
        "text_q": draw_text_q(jax.random.fold_in(splits[8], 71), 0),
        "text_k": draw_text_k(jax.random.fold_in(splits[8], 71), 0),
        "text_v": gaussian(splits[5], (TXT, D), 1.0, 6.0, ((1, 2),)),
        "text_len": jax.random.randint(splits[6], (1,), TXT // 2, TXT + 1).astype(jnp.int32),
        "win_start": draw_win_start(jax.random.fold_in(splits[8], 71), 0),
    }


def reference(video_q, video_k, video_v, text_q, text_k, text_v, text_len, win_start):
    tile_rows = TT * TH * TW
    slab_rows = tile_rows * GH * GW
    window_rows = KW * tile_rows
    reach = KT // 2
    frame_tiles = N_WIDE
    score_scale = HDIM ** -0.5
    blank_slab = jnp.zeros((reach * slab_rows, HEADS * HDIM), jnp.bfloat16)
    keys_padded = jnp.concatenate([blank_slab, video_k, blank_slab], 0)
    values_padded = jnp.concatenate([blank_slab, video_v, blank_slab], 0)
    text_usable = jnp.arange(TXT) < text_len[0]
    text_keys = text_k.astype(jnp.float32).reshape(TXT, HEADS, HDIM)
    text_values = text_v.astype(jnp.float32).reshape(TXT, HEADS, HDIM)

    def one_tile(tile_index):
        frame = tile_index // (GH * GW)
        inside = tile_index % (GH * GW)
        tile_row = inside // GW
        offset = (tile_row * GW + win_start[tile_index]) * tile_rows
        queries = lax.dynamic_slice_in_dim(video_q, (tile_index * tile_rows).astype(jnp.int32), tile_rows, 0)
        queries = queries.astype(jnp.float32).reshape(tile_rows, HEADS, HDIM)
        key_parts = []
        value_parts = []
        usable_parts = []
        for depth in range(KT):
            begin = ((frame + depth) * slab_rows + offset).astype(jnp.int32)
            key_parts.append(lax.dynamic_slice_in_dim(keys_padded, begin, window_rows, 0))
            value_parts.append(lax.dynamic_slice_in_dim(values_padded, begin, window_rows, 0))
            exists = (frame + depth - reach >= 0) & (frame + depth - reach < frame_tiles)
            usable_parts.append(jnp.broadcast_to(exists, (window_rows,)))
        key_block = jnp.concatenate(key_parts, 0).astype(jnp.float32).reshape(-1, HEADS, HDIM)
        value_block = jnp.concatenate(value_parts, 0).astype(jnp.float32).reshape(-1, HEADS, HDIM)
        key_block = jnp.concatenate([key_block, text_keys], 0)
        value_block = jnp.concatenate([value_block, text_values], 0)
        usable = jnp.concatenate(usable_parts + [text_usable], 0)
        scores = jnp.einsum('qhd,khd->hqk', queries, key_block) * score_scale
        scores = jnp.where(usable[None, None, :], scores, -jnp.inf)
        peak = jnp.max(scores, axis=-1, keepdims=True)
        weights = jnp.exp(scores - peak)
        denom = jnp.sum(weights, axis=-1)
        probs = weights.astype(jnp.bfloat16).astype(jnp.float32)
        mixed = jnp.einsum('hqk,khd->qhd', probs, value_block)
        result = mixed / jnp.transpose(denom)[:, :, None]
        return result.reshape(tile_rows, HEADS * HDIM).astype(jnp.bfloat16)

    attended = lax.map(one_tile, jnp.arange(frame_tiles * GH * GW, dtype=jnp.int32))
    video_out = attended.reshape(frame_tiles * slab_rows, HEADS * HDIM)

    text_queries = text_q.astype(jnp.float32).reshape(TXT, HEADS, HDIM)

    def one_slab(frame):
        begin = (frame * slab_rows).astype(jnp.int32)
        key_block = lax.dynamic_slice_in_dim(video_k, begin, slab_rows, 0).astype(jnp.float32).reshape(slab_rows, HEADS, HDIM)
        value_block = lax.dynamic_slice_in_dim(video_v, begin, slab_rows, 0).astype(jnp.float32).reshape(slab_rows, HEADS, HDIM)
        scores = jnp.einsum('qhd,khd->hqk', text_queries, key_block) * score_scale
        peak = jnp.max(scores, axis=-1)
        weights = jnp.exp(scores - peak[:, :, None])
        totals = jnp.sum(weights, axis=-1)
        probs = weights.astype(jnp.bfloat16).astype(jnp.float32)
        accumulated = jnp.einsum('hqk,khd->qhd', probs, value_block)
        return peak, totals, accumulated

    tile_peak, tile_sum, tile_acc = lax.map(one_slab, jnp.arange(frame_tiles, dtype=jnp.int32))
    self_scores = jnp.einsum('qhd,khd->hqk', text_queries, text_keys) * score_scale
    self_scores = jnp.where(text_usable[None, None, :], self_scores, -jnp.inf)
    self_peak = jnp.max(self_scores, axis=-1)
    self_weights = jnp.exp(self_scores - self_peak[:, :, None])
    self_sum = jnp.sum(self_weights, axis=-1)
    self_probs = self_weights.astype(jnp.bfloat16).astype(jnp.float32)
    self_acc = jnp.einsum('hqk,khd->qhd', self_probs, text_values)
    ceiling = jnp.maximum(jnp.max(tile_peak, axis=0), self_peak)
    tile_scale = jnp.exp(tile_peak - ceiling[None])
    self_scale = jnp.exp(self_peak - ceiling)
    numerator = jnp.sum(jnp.transpose(tile_scale, (0, 2, 1))[:, :, :, None] * tile_acc, axis=0)
    numerator = numerator + jnp.transpose(self_scale)[:, :, None] * self_acc
    denominator = jnp.sum(tile_scale * tile_sum, axis=0) + self_scale * self_sum
    text_out = (numerator / jnp.transpose(denominator)[:, :, None]).reshape(TXT, HEADS * HDIM).astype(jnp.bfloat16)
    return video_out, text_out
```

```python
import functools

import jax
import jax.numpy as jnp
from jax import lax
from jax.experimental import pallas as pl
from jax.experimental.pallas import tpu as pltpu
from jax.sharding import PartitionSpec as P

HDIM = 128
TT = 6
TH = 8
TW = 8
GH = 2
GW = 3
KT = 3
KW = 2
TXT = 256


def extended(cells, sides, width):
    for axis, dim in sides:
        count = lax.axis_size(axis)
        ends = count - 1
        head = lax.slice_in_dim(cells, 0, width, axis=dim)
        tail = lax.slice_in_dim(cells, cells.shape[dim] - width, cells.shape[dim], axis=dim)
        cells = jnp.concatenate(
            [
                lax.ppermute(tail, axis, [(i, (i + 1) % count) for i in range(ends)]),
                cells,
                lax.ppermute(head, axis, [((i + 1) % count, i) for i in range(ends)]),
            ],
            axis=dim,
        )
    return cells


def softmax_parts(queries, key_block, value_block, usable, score_scale):
    scores = (
        jnp.einsum("qhd,khd->hqk", queries, key_block, preferred_element_type=jnp.float32)
        * score_scale
    )
    if usable is not None:
        scores = jnp.where(usable[None, None, :], scores, -jnp.inf)
    peak = jnp.max(scores, axis=-1)
    weights = jnp.exp(scores - peak[:, :, None])
    totals = jnp.sum(weights, axis=-1)
    probs = weights.astype(jnp.bfloat16)
    accumulated = jnp.einsum("hqk,khd->qhd", probs, value_block, preferred_element_type=jnp.float32)
    return (peak, totals, accumulated)


def split_heads(video_q, video_k, video_v, text_q, text_k, text_v, text_len, win_start):
    features = text_q.shape[1]
    local_heads = features // HDIM
    slab_count = lax.axis_size("wide")
    position = lax.axis_index("wide")
    slab_rows = video_q.shape[0] * lax.axis_size("narrow")
    tile_rows = TT * TH * TW
    tiles_here = slab_rows // tile_rows
    window_rows = KW * tile_rows
    reach = KT // 2
    score_scale = HDIM ** (-0.5)
    key_value = jnp.stack([video_k, video_v])
    query_set, pair_set = (
        lax.all_to_all(video_q[None], "narrow", split_axis=2, concat_axis=1, tiled=True),
        lax.all_to_all(key_value, "narrow", split_axis=2, concat_axis=1, tiled=True),
    )
    queries_all = query_set[0]
    beside_all = extended(pair_set[:, None], (("wide", 1),), reach)
    stacked = beside_all.reshape(2, KT * slab_rows, features)
    own_slab = beside_all[:, reach]
    text_pair = jnp.stack([text_k, text_v])
    text_usable = jnp.arange(TXT) < text_len[0]
    usable_parts = []
    for depth in range(KT):
        exists = (position + depth - reach >= 0) & (position + depth - reach < slab_count)
        usable_parts.append(jnp.broadcast_to(exists, (window_rows,)))
    usable = jnp.concatenate(usable_parts + [text_usable], 0)
    starts = lax.dynamic_slice_in_dim(win_start, position * tiles_here, tiles_here)

    def one_tile(entry):
        which, first_col = entry
        tile_row = which // GW
        offset = (tile_row * GW + first_col) * tile_rows
        pieces = [
            lax.dynamic_slice_in_dim(stacked, depth * slab_rows + offset, window_rows, 1)
            for depth in range(KT)
        ]
        key_block = jnp.concatenate(pieces + [text_pair], 1).reshape(2, -1, local_heads, HDIM)
        queries = lax.dynamic_slice_in_dim(queries_all, which * tile_rows, tile_rows, 0).reshape(
            tile_rows, local_heads, HDIM
        )
        peak, totals, accumulated = softmax_parts(
            queries, key_block[0], key_block[1], usable, score_scale
        )
        result = accumulated / jnp.transpose(totals)[:, :, None]
        return result.reshape(tile_rows, features).astype(jnp.bfloat16)

    attended = lax.map(one_tile, (jnp.arange(tiles_here, dtype=jnp.int32), starts))
    attended = attended.reshape(slab_rows, features)
    video_out = lax.all_to_all(attended, "narrow", split_axis=0, concat_axis=1, tiled=True)
    text_queries = text_q.reshape(TXT, local_heads, HDIM)
    slab_keys = own_slab[0].reshape(slab_rows, local_heads, HDIM)
    slab_values = own_slab[1].reshape(slab_rows, local_heads, HDIM)
    tile_peak, tile_sum, tile_acc = softmax_parts(
        text_queries, slab_keys, slab_values, None, score_scale
    )
    ceiling = lax.pmax(tile_peak, "wide")
    rescale = jnp.exp(tile_peak - ceiling)
    totals, accumulated = lax.psum(
        (rescale * tile_sum, jnp.transpose(rescale)[:, :, None] * tile_acc), "wide"
    )
    text_keys = text_k.reshape(TXT, local_heads, HDIM)
    text_values = text_v.reshape(TXT, local_heads, HDIM)
    self_peak, self_sum, self_acc = softmax_parts(
        text_queries, text_keys, text_values, text_usable, score_scale
    )
    top = jnp.maximum(ceiling, self_peak)
    video_scale = jnp.exp(ceiling - top)
    self_scale = jnp.exp(self_peak - top)
    numerator = (
        jnp.transpose(video_scale)[:, :, None] * accumulated
        + jnp.transpose(self_scale)[:, :, None] * self_acc
    )
    denominator = video_scale * totals + self_scale * self_sum
    text_out = (
        (numerator / jnp.transpose(denominator)[:, :, None])
        .reshape(TXT, features)
        .astype(jnp.bfloat16)
    )
    return (video_out, text_out)


TILE = TT * TH * TW
WINDOW = KW * TILE
ROW = GW * TILE
EXP2_SCALE = HDIM**-0.5 * 1.4426950408889634
SLOT = 2
BY_ROWS = (((1,), (1,)), ((), ()))
PLAIN = (((1,), (0,)), ((), ()))
BY_COLS = (((0,), (0,)), ((), ()))


def dot(a, b, dims):
    return lax.dot_general(a, b, dims, preferred_element_type=jnp.float32)


def video_kernel(info, q, k, v, before, after, text_k, text_v, _, out):
    has_before, has_after, text_len = info[GW] == 1, info[GW + 1] == 1, info[GW + 2]
    usable = lax.broadcasted_iota(jnp.int32, (TILE, TXT), 1) < text_len
    for tile in range(GW):
        rows = pl.ds(tile * TILE, TILE)
        window = pl.ds(pl.multiple_of(info[tile] * TILE, TILE), WINDOW)
        own = k[window, :]
        keys = [
            text_k[...],
            own,
            jnp.where(has_before, before[0, window, :], own),
            jnp.where(has_after, after[0, window, :], own),
        ]
        values = [text_v[...], v[window, :], before[1, window, :], after[1, window, :]]
        counts = [None, None, has_before, has_after]
        queries = q[rows, :]
        scores = [dot(queries, block, BY_ROWS) for block in keys]
        scores[0] = jnp.where(usable, scores[0], -jnp.inf)
        peak = functools.reduce(
            jnp.maximum, [jnp.max(block, axis=1, keepdims=True) for block in scores]
        )
        total = jnp.zeros((TILE, 1), jnp.float32)
        mixed = jnp.zeros((TILE, HDIM), jnp.float32)
        for block, value, counted in zip(scores, values, counts):
            weights = jnp.exp2((block - peak) * EXP2_SCALE)
            part = jnp.sum(weights, axis=1, keepdims=True)
            total += part if counted is None else jnp.where(counted, part, 0.0)
            mixed += dot(weights.astype(jnp.bfloat16), value, PLAIN)
        out[rows, :] = (mixed / total).astype(jnp.bfloat16)


def video_slot(first, heads, info, q, k, v, before, after, text_k, text_v, out):
    own = pl.BlockSpec((ROW, HDIM), lambda h, _: (0, first + h))
    halo = pl.BlockSpec((2, ROW, HDIM), lambda h, _: (0, 0, h))
    text = pl.BlockSpec((TXT, HDIM), lambda h, _: (0, first + h))
    keys = KT * WINDOW + TXT
    return pl.pallas_call(
        video_kernel,
        grid_spec=pltpu.PrefetchScalarGridSpec(
            num_scalar_prefetch=1,
            grid=(heads,),
            in_specs=[own, own, own, halo, halo, text, text, pl.BlockSpec(memory_space=pl.ANY)],
            out_specs=own,
        ),
        out_shape=jax.ShapeDtypeStruct(q.shape, jnp.bfloat16),
        input_output_aliases={8: 0},
        compiler_params=pltpu.CompilerParams(vmem_limit_bytes=48 * 2**20),
        cost_estimate=pl.CostEstimate(
            flops=heads * ROW * keys * HDIM * 4,
            bytes_accessed=heads * ROW * HDIM * 16,
            transcendentals=heads * ROW * keys,
        ),
        name="video_attention",
    )(info, q, k, v, before, after, text_k, text_v, out)


def text_kernel(info, text_q, k, v, text_k, text_v, peak, total, mixed):
    def part(keys, values, usable):
        scores = dot(keys, text_q[...], BY_ROWS)
        if usable is not None:
            scores = jnp.where(usable, scores, -jnp.inf)
        top = jnp.max(scores, axis=0, keepdims=True)
        weights = jnp.exp2((scores - top) * EXP2_SCALE)
        return (
            top,
            jnp.sum(weights, axis=0, keepdims=True),
            dot(values, weights.astype(jnp.bfloat16), BY_COLS),
        )

    video = part(k[...], v[...], None)
    peak[0], total[0], mixed[0] = video

    @pl.when(info[GW + 3] == 1)
    def _():
        usable = lax.broadcasted_iota(jnp.int32, (TXT, TXT), 0) < info[GW + 2]
        own = part(text_k[...], text_v[...], usable)
        top = jnp.maximum(peak[0], own[0])
        scale = jnp.exp2((peak[0] - top) * EXP2_SCALE)
        own_scale = jnp.exp2((own[0] - top) * EXP2_SCALE)
        peak[0] = top
        total[0] = scale * total[0] + own_scale * own[1]
        mixed[0] = scale * mixed[0] + own_scale * own[2]


def text_parts(info, text_q, k, v, text_k, text_v):
    heads = k.shape[1] // HDIM
    own = pl.BlockSpec((ROW, HDIM), lambda h, _: (0, h))
    text = pl.BlockSpec((TXT, HDIM), lambda h, _: (0, h))
    row = pl.BlockSpec((1, 1, TXT), lambda h, _: (h, 0, 0))
    return pl.pallas_call(
        text_kernel,
        grid_spec=pltpu.PrefetchScalarGridSpec(
            num_scalar_prefetch=1,
            grid=(heads,),
            in_specs=[text, own, own, text, text],
            out_specs=[row, row, pl.BlockSpec((1, HDIM, TXT), lambda h, _: (h, 0, 0))],
        ),
        out_shape=[
            jax.ShapeDtypeStruct((heads, 1, TXT), jnp.float32),
            jax.ShapeDtypeStruct((heads, 1, TXT), jnp.float32),
            jax.ShapeDtypeStruct((heads, HDIM, TXT), jnp.float32),
        ],
        compiler_params=pltpu.CompilerParams(vmem_limit_bytes=48 * 2**20),
        cost_estimate=pl.CostEstimate(
            flops=heads * ROW * TXT * HDIM * 4,
            bytes_accessed=heads * (ROW + TXT) * HDIM * 4,
            transcendentals=heads * ROW * TXT,
        ),
        name="text_attention",
    )(info, text_q, k, v, text_k, text_v)


def keep_rows(video_q, video_k, video_v, text_q, text_k, text_v, text_len, win_start):
    features = video_q.shape[1]
    heads = features // HDIM
    count = lax.axis_size("wide")
    frame, row = lax.axis_index("wide"), lax.axis_index("narrow")
    forward = [(i, i + 1) for i in range(count - 1)]
    backward = [(i + 1, i) for i in range(count - 1)]
    starts = lax.dynamic_slice_in_dim(win_start, (frame * GH + row) * GW, GW)
    info = jnp.concatenate(
        [
            starts,
            jnp.stack([frame > 0, frame < count - 1]).astype(jnp.int32),
            text_len,
            ((frame == 0) & (row == 0)).astype(jnp.int32)[None],
        ]
    )
    texts = lax.all_gather(
        jnp.stack([text_q, text_k, text_v]), "narrow", axis=2, tiled=True
    )
    text_q, text_k, text_v = texts[0], texts[1], texts[2]
    halos = []
    for first in range(0, heads, SLOT):
        columns = slice(first * HDIM, (first + SLOT) * HDIM)
        pair = jnp.stack([video_k[:, columns], video_v[:, columns]])
        halos.append(
            (lax.ppermute(pair, "wide", forward), lax.ppermute(pair, "wide", backward))
        )
    peak, total, mixed = text_parts(info, text_q, video_k, video_v, text_k, text_v)
    top = lax.pmax(peak, ("wide", "narrow"))
    scale = jnp.exp2((peak - top) * EXP2_SCALE)
    total, mixed = lax.psum_scatter(
        (scale * total, scale * mixed), "narrow", scatter_dimension=0, tiled=True
    )
    total, mixed = lax.psum((total, mixed), "wide")
    text_out = (
        jnp.transpose(mixed / total, (2, 0, 1)).reshape(TXT, -1).astype(jnp.bfloat16)
    )
    out = jnp.zeros(video_q.shape, jnp.bfloat16)
    for slot, (before, after) in enumerate(halos):
        out = video_slot(
            slot * SLOT, SLOT, info, video_q, video_k, video_v, before, after, text_k, text_v, out
        )
    return out, text_out


def solution(mesh):
    tokens = P(("wide", "narrow"), None)
    text = P(None, "narrow")
    body = keep_rows if mesh.shape["narrow"] == GH else split_heads
    return jax.shard_map(
        body,
        mesh=mesh,
        in_specs=(tokens, tokens, tokens, text, text, text, P(), P()),
        out_specs=(tokens, text),
        check_vma=False,
    )
```

```python
import functools

import jax
import jax.numpy as jnp
from jax import lax
from jax.experimental import pallas as pl
from jax.experimental.pallas import tpu as pltpu
from jax.sharding import PartitionSpec as P

HDIM = 128
TT = 6
TH = 8
TW = 8
GH = 2
GW = 3
KT = 3
KW = 2
TXT = 256


def extended(cells, sides, width):
    for axis, dim in sides:
        count = lax.axis_size(axis)
        ends = count - 1
        head = lax.slice_in_dim(cells, 0, width, axis=dim)
        tail = lax.slice_in_dim(cells, cells.shape[dim] - width, cells.shape[dim], axis=dim)
        cells = jnp.concatenate(
            [
                lax.ppermute(tail, axis, [(i, (i + 1) % count) for i in range(ends)]),
                cells,
                lax.ppermute(head, axis, [((i + 1) % count, i) for i in range(ends)]),
            ],
            axis=dim,
        )
    return cells


def softmax_parts(queries, key_block, value_block, usable, score_scale):
    scores = (
        jnp.einsum("qhd,khd->hqk", queries, key_block, preferred_element_type=jnp.float32)
        * score_scale
    )
    if usable is not None:
        scores = jnp.where(usable[None, None, :], scores, -jnp.inf)
    peak = jnp.max(scores, axis=-1)
    weights = jnp.exp(scores - peak[:, :, None])
    totals = jnp.sum(weights, axis=-1)
    probs = weights.astype(jnp.bfloat16)
    accumulated = jnp.einsum("hqk,khd->qhd", probs, value_block, preferred_element_type=jnp.float32)
    return (peak, totals, accumulated)


def split_heads(video_q, video_k, video_v, text_q, text_k, text_v, text_len, win_start):
    features = text_q.shape[1]
    local_heads = features // HDIM
    slab_count = lax.axis_size("wide")
    position = lax.axis_index("wide")
    slab_rows = video_q.shape[0] * lax.axis_size("narrow")
    tile_rows = TT * TH * TW
    tiles_here = slab_rows // tile_rows
    window_rows = KW * tile_rows
    reach = KT // 2
    score_scale = HDIM ** (-0.5)
    key_value = jnp.stack([video_k, video_v])
    query_set, pair_set = (
        lax.all_to_all(video_q[None], "narrow", split_axis=2, concat_axis=1, tiled=True),
        lax.all_to_all(key_value, "narrow", split_axis=2, concat_axis=1, tiled=True),
    )
    queries_all = query_set[0]
    beside_all = extended(pair_set[:, None], (("wide", 1),), reach)
    stacked = beside_all.reshape(2, KT * slab_rows, features)
    own_slab = beside_all[:, reach]
    text_pair = jnp.stack([text_k, text_v])
    text_usable = jnp.arange(TXT) < text_len[0]
    usable_parts = []
    for depth in range(KT):
        exists = (position + depth - reach >= 0) & (position + depth - reach < slab_count)
        usable_parts.append(jnp.broadcast_to(exists, (window_rows,)))
    usable = jnp.concatenate(usable_parts + [text_usable], 0)
    starts = lax.dynamic_slice_in_dim(win_start, position * tiles_here, tiles_here)

    def one_tile(entry):
        which, first_col = entry
        tile_row = which // GW
        offset = (tile_row * GW + first_col) * tile_rows
        pieces = [
            lax.dynamic_slice_in_dim(stacked, depth * slab_rows + offset, window_rows, 1)
            for depth in range(KT)
        ]
        key_block = jnp.concatenate(pieces + [text_pair], 1).reshape(2, -1, local_heads, HDIM)
        queries = lax.dynamic_slice_in_dim(queries_all, which * tile_rows, tile_rows, 0).reshape(
            tile_rows, local_heads, HDIM
        )
        peak, totals, accumulated = softmax_parts(
            queries, key_block[0], key_block[1], usable, score_scale
        )
        result = accumulated / jnp.transpose(totals)[:, :, None]
        return result.reshape(tile_rows, features).astype(jnp.bfloat16)

    attended = lax.map(one_tile, (jnp.arange(tiles_here, dtype=jnp.int32), starts))
    attended = attended.reshape(slab_rows, features)
    video_out = lax.all_to_all(attended, "narrow", split_axis=0, concat_axis=1, tiled=True)
    text_queries = text_q.reshape(TXT, local_heads, HDIM)
    slab_keys = own_slab[0].reshape(slab_rows, local_heads, HDIM)
    slab_values = own_slab[1].reshape(slab_rows, local_heads, HDIM)
    tile_peak, tile_sum, tile_acc = softmax_parts(
        text_queries, slab_keys, slab_values, None, score_scale
    )
    ceiling = lax.pmax(tile_peak, "wide")
    rescale = jnp.exp(tile_peak - ceiling)
    totals, accumulated = lax.psum(
        (rescale * tile_sum, jnp.transpose(rescale)[:, :, None] * tile_acc), "wide"
    )
    text_keys = text_k.reshape(TXT, local_heads, HDIM)
    text_values = text_v.reshape(TXT, local_heads, HDIM)
    self_peak, self_sum, self_acc = softmax_parts(
        text_queries, text_keys, text_values, text_usable, score_scale
    )
    top = jnp.maximum(ceiling, self_peak)
    video_scale = jnp.exp(ceiling - top)
    self_scale = jnp.exp(self_peak - top)
    numerator = (
        jnp.transpose(video_scale)[:, :, None] * accumulated
        + jnp.transpose(self_scale)[:, :, None] * self_acc
    )
    denominator = video_scale * totals + self_scale * self_sum
    text_out = (
        (numerator / jnp.transpose(denominator)[:, :, None])
        .reshape(TXT, features)
        .astype(jnp.bfloat16)
    )
    return (video_out, text_out)


TILE = TT * TH * TW
WINDOW = KW * TILE
ROW = GW * TILE
EXP2_SCALE = HDIM**-0.5 * 1.4426950408889634
QUAD = 4
SLOTS = (
    (1, 0), (2, 0), (3, 1), (3, 2), (3, 3), (3, 1), (3, 2), (3, 3), (2, 0), (1, 0),
)
AHEAD = 3
BY_ROWS = (((1,), (1,)), ((), ()))
PLAIN = (((1,), (0,)), ((), ()))
BY_COLS = (((0,), (0,)), ((), ()))
ANY = pl.BlockSpec(memory_space=pl.ANY)


def dot(a, b, dims):
    return lax.dot_general(a, b, dims, preferred_element_type=jnp.float32)


def core_pairs(count):
    return [(i, i ^ 1) for i in range(count)]


def mirrored(count, pairs):
    return pairs + [(count - 1 - a, count - 1 - b) for a, b in pairs]


def chip_pairs(count, kind):
    pairs = [(i, i + 1) for i in range(1, count - 1, QUAD)]
    for z in range(count // QUAD - 1):
        end = QUAD * z + QUAD - 1
        pairs.append((end, QUAD * z if z < kind else end + 1))
    return mirrored(count, pairs)


def relay_pairs(count, kind):
    rows = count // QUAD
    return mirrored(count, [(QUAD * z, QUAD * z + QUAD) for z in range(min(kind, rows - 1))])


def pack_kernel(place, k, v, pair):
    pair[0], pair[1] = k[...], v[...]


def rotated(first, row, heads):
    return (first + row * (heads // GH)) % heads


def pack(first, heads, scalars, k, v):
    every = k.shape[1] // HDIM
    own = pl.BlockSpec((ROW, HDIM), lambda h, place: (0, rotated(first, place[1], every) + h))
    return pl.pallas_call(
        pack_kernel,
        grid_spec=pltpu.PrefetchScalarGridSpec(
            num_scalar_prefetch=1,
            grid=(heads,),
            in_specs=[own, own],
            out_specs=pl.BlockSpec((2, ROW, HDIM), lambda h, _: (0, 0, h)),
        ),
        out_shape=jax.ShapeDtypeStruct((2, ROW, heads * HDIM), k.dtype),
        cost_estimate=pl.CostEstimate(
            flops=0, bytes_accessed=heads * ROW * HDIM * 8, transcendentals=0
        ),
        name="pack_slot",
    )(scalars[-1], k, v)


def video_kernel(kind, rows, packs, win_start, text_len, place, q, k, v, *rest):
    near_k, near_v, far, text_k, text_v = rest[:5]
    relay = rest[5] if kind else None
    frame, row = place[0], place[1]
    z, at = frame // QUAD, frame % QUAD
    has_far = (frame > 0) & (frame < rows * QUAD - 1)
    relayed = ((at == 0) & (z <= kind)) | ((at == QUAD - 1) & (z >= rows - 1 - kind))
    usable = lax.broadcasted_iota(jnp.int32, (TILE, TXT), 1) < text_len[0]
    if packs:
        next_k, next_v = rest[5 + bool(kind) :][:2]
        pair = rest[-1]
        pair[0], pair[1] = next_k[...], next_v[...]
    out = rest[-2] if packs else rest[-1]

    for tile in range(GW):
        here = pl.ds(tile * TILE, TILE)
        start = win_start[(frame * GH + row) * GW + tile]
        window = pl.ds(pl.multiple_of(start * TILE, TILE), WINDOW)
        own = k[window, :]
        far_k, far_v = far[0, window, :], far[1, window, :]
        if kind:
            far_k = jnp.where(relayed, relay[0, window, :], far_k)
            far_v = jnp.where(relayed, relay[1, window, :], far_v)
        keys = [text_k[...], own, near_k[window, :], jnp.where(has_far, far_k, own)]
        values = [text_v[...], v[window, :], near_v[window, :], far_v]
        queries = q[here, :]
        scores = [dot(queries, block, BY_ROWS) for block in keys]
        scores[0] = jnp.where(usable, scores[0], -jnp.inf)
        peak = functools.reduce(
            jnp.maximum, [jnp.max(block, axis=1, keepdims=True) for block in scores]
        )
        mixed = jnp.zeros((TILE, HDIM), jnp.float32)
        sums = []
        for block, value in zip(scores, values):
            weights = jnp.exp2((block - peak) * EXP2_SCALE)
            sums.append(jnp.sum(weights, axis=1, keepdims=True))
            mixed += dot(weights.astype(jnp.bfloat16), value, PLAIN)
        total = sums[0] + sums[1] + sums[2] + jnp.where(has_far, sums[3], 0.0)
        out[here, :] = (mixed / total).astype(jnp.bfloat16)


def video_slot(first, heads, kind, rows, scalars, q, k, v, near, far, text, following, gates, out):
    every = q.shape[1] // HDIM

    def columns(first, per, last):
        return pl.BlockSpec(
            (ROW, per * HDIM),
            lambda h, *s: (0, rotated(first, s[2][1], every) // per + jnp.minimum(h, last)),
        )

    own = columns(first, 1, heads - 1)
    halo = pl.BlockSpec((2, ROW, HDIM), lambda h, *_: (0, 0, h))
    prompt = pl.BlockSpec((TXT, HDIM), lambda h, *_: (0, first % (every // GH) + h))
    keys = KT * WINDOW + TXT
    inputs = [q, k, v, *near, far[0], *text]
    specs = [own] * 5 + [halo, prompt, prompt]
    if kind:
        inputs, specs = inputs + [far[1]], specs + [halo]
    out_specs = [own]
    out_shape = [jax.ShapeDtypeStruct(q.shape, q.dtype)]
    if following:
        next_first, next_heads = following
        per = 1 if next_heads <= heads else next_heads
        last = next_heads // per - 1
        inputs = inputs + [k, v]
        specs = specs + [columns(next_first, per, last)] * 2
        out_specs.append(
            pl.BlockSpec((2, ROW, per * HDIM), lambda h, *_: (0, 0, jnp.minimum(h, last)))
        )
        out_shape.append(jax.ShapeDtypeStruct((2, ROW, next_heads * HDIM), k.dtype))
    inputs, specs = inputs + list(gates), specs + [ANY] * len(gates)
    aliases = {}
    if out is not None:
        inputs, specs = inputs + [out], specs + [ANY]
        aliases = {len(scalars) + len(inputs) - 1: 0}
    return pl.pallas_call(
        functools.partial(video_kernel, kind, rows, bool(following)),
        grid_spec=pltpu.PrefetchScalarGridSpec(
            num_scalar_prefetch=len(scalars),
            grid=(heads,),
            in_specs=specs,
            out_specs=out_specs,
        ),
        out_shape=out_shape,
        input_output_aliases=aliases,
        compiler_params=pltpu.CompilerParams(vmem_limit_bytes=48 * 2**20),
        cost_estimate=pl.CostEstimate(
            flops=heads * ROW * keys * HDIM * 4,
            bytes_accessed=heads * ROW * HDIM * 16,
            transcendentals=heads * ROW * keys,
        ),
        name="video_attention",
    )(*scalars, *inputs)


def text_sums_kernel(text_q, k, v, usable, stats, mixed):
    scores = dot(k, text_q, BY_ROWS)
    if usable is not None:
        scores = jnp.where(usable, scores, -jnp.inf)
    top = jnp.max(scores, axis=0, keepdims=True)
    weights = jnp.exp2((scores - top) * EXP2_SCALE)
    stats[0, 0:1], stats[0, 1:2] = top, jnp.sum(weights, axis=0, keepdims=True)
    sums = dot(v, weights.astype(jnp.bfloat16), BY_COLS)
    mixed[:, 0] = sums.reshape(mixed.shape[0], HDIM // mixed.shape[0], TXT)


def text_video_kernel(half, place, local_q, remote_q, k, v, *rest):
    queries = jnp.where(pl.program_id(0) < half, local_q[...], remote_q[...])
    text_sums_kernel(queries, k[...], v[...], None, *rest[-2:])


def text_own_kernel(text_len, text_q, text_k, text_v, stats, mixed):
    usable = lax.broadcasted_iota(jnp.int32, (TXT, TXT), 0) < text_len[0]
    text_sums_kernel(text_q[...], text_k[...], text_v[...], usable, stats, mixed)


def text_video(shares, scalars, local_q, remote_q, k, v, gates):
    heads = k.shape[1] // HDIM
    half = heads // GH
    depth = HDIM // shares

    def head(h, place):
        return (h + place[1] * half) % heads

    own = pl.BlockSpec((ROW, HDIM), lambda h, place: (0, head(h, place)))
    return pl.pallas_call(
        functools.partial(text_video_kernel, half),
        grid_spec=pltpu.PrefetchScalarGridSpec(
            num_scalar_prefetch=1,
            grid=(heads,),
            in_specs=[
                pl.BlockSpec((TXT, HDIM), lambda h, _: (0, jnp.minimum(h, half - 1))),
                pl.BlockSpec((TXT, HDIM), lambda h, _: (0, jnp.maximum(h - half, 0))),
                own,
                own,
            ]
            + [ANY] * len(gates),
            out_specs=[
                pl.BlockSpec((1, 2, TXT), lambda h, place: (head(h, place), 0, 0)),
                pl.BlockSpec(
                    (shares, 1, depth, TXT),
                    lambda h, place: (head(h, place) // half, h % half, 0, 0),
                ),
            ],
        ),
        out_shape=[
            jax.ShapeDtypeStruct((heads, 2, TXT), jnp.float32),
            jax.ShapeDtypeStruct((GH * shares, half, depth, TXT), jnp.float32),
        ],
        compiler_params=pltpu.CompilerParams(vmem_limit_bytes=48 * 2**20),
        cost_estimate=pl.CostEstimate(
            flops=heads * ROW * TXT * HDIM * 4,
            bytes_accessed=heads * (ROW + TXT) * HDIM * 4,
            transcendentals=heads * ROW * TXT,
        ),
        name="text_over_video",
    )(scalars[-1], local_q, remote_q, k, v, *gates)


def text_own(shares, text_len, text_q, text_k, text_v):
    heads = text_q.shape[1] // HDIM
    depth = HDIM // shares
    text = pl.BlockSpec((TXT, HDIM), lambda h, _: (0, h))
    return pl.pallas_call(
        text_own_kernel,
        grid_spec=pltpu.PrefetchScalarGridSpec(
            num_scalar_prefetch=1,
            grid=(heads,),
            in_specs=[text] * 3,
            out_specs=[
                pl.BlockSpec((1, 2, TXT), lambda h, _: (h, 0, 0)),
                pl.BlockSpec((shares, 1, depth, TXT), lambda h, _: (0, h, 0, 0)),
            ],
        ),
        out_shape=[
            jax.ShapeDtypeStruct((heads, 2, TXT), jnp.float32),
            jax.ShapeDtypeStruct((shares, heads, depth, TXT), jnp.float32),
        ],
        cost_estimate=pl.CostEstimate(
            flops=heads * TXT * TXT * HDIM * 4,
            bytes_accessed=heads * TXT * HDIM * 10,
            transcendentals=heads * TXT * TXT,
        ),
        name="text_over_text",
    )(text_len, text_q, text_k, text_v)


def finish_kernel(place, both, share, other, own_both, own_share, *rest):
    def parts(ref):
        return ref[:, 0:1, :], ref[:, 1:2, :]

    top, total = parts(both)
    own_top, own_total = parts(own_both)
    peak = jnp.maximum(top, own_top)
    scale = jnp.exp2((top - peak) * EXP2_SCALE)
    own_scale = jnp.exp2((own_top - peak) * EXP2_SCALE)
    mixed = scale * (share[...] + other[...]) + own_scale * own_share[0]
    rest[-1][...] = mixed / (scale * total + own_scale * own_total)


def finish(scalars, both, share, other, own_both, own_mixed, gates):
    half, depth, queries = other.shape
    local = pl.BlockSpec((half, depth, queries), lambda i, *_: (0, 0, 0))
    return pl.pallas_call(
        finish_kernel,
        grid_spec=pltpu.PrefetchScalarGridSpec(
            num_scalar_prefetch=1,
            grid=(1,),
            in_specs=[
                pl.BlockSpec((half, 2, queries), lambda i, place: (place[1], 0, 0)),
                pl.BlockSpec((half, depth, queries), lambda i, place: (0, place[3], 0)),
                local,
                pl.BlockSpec((half, 2, queries), lambda i, *_: (0, 0, 0)),
                pl.BlockSpec(
                    (1, half, depth, queries), lambda i, place: (place[2], 0, place[3], 0)
                ),
            ]
            + [ANY] * len(gates),
            out_specs=local,
        ),
        out_shape=jax.ShapeDtypeStruct(other.shape, jnp.float32),
        name="finish_text",
    )(scalars[-1], both, share, other, own_both, own_mixed, *gates)


def text_sums(count, stats, mixed, every):
    shares = count // 2
    half = mixed.shape[1]
    groups = [[n * count + i for n in range(GH) for i in column] for column in columns(count)]
    peaks, totals = every[:, :, 0], every[:, :, 1]
    top = jnp.max(peaks, axis=0)
    total = jnp.sum(jnp.exp2((peaks - top) * EXP2_SCALE) * totals, axis=0)
    scale = jnp.exp2((stats[:, 0] - top) * EXP2_SCALE).reshape(GH, 1, half, 1, TXT)
    scaled = scale * mixed.reshape(GH, shares, half, -1, TXT)
    share = lax.psum_scatter(
        scaled.reshape(mixed.shape),
        ("narrow", "wide"),
        scatter_dimension=0,
        axis_index_groups=groups,
    )
    return jnp.stack([top, total], 1), share


def columns(count):
    return [[i for i in range(count) if i % QUAD // 2 == x] for x in range(2)]


def hold_kernel(block, gate, out):
    pass


def hold(block, gate):
    return pl.pallas_call(
        hold_kernel,
        in_specs=[ANY, ANY],
        out_specs=ANY,
        out_shape=jax.ShapeDtypeStruct(block.shape, block.dtype),
        input_output_aliases={0: 0},
        name="hold_slot",
    )(block, gate)


def keep_rows(video_q, video_k, video_v, text_q, text_k, text_v, text_len, win_start):
    count = lax.axis_size("wide")
    rows = count // QUAD
    frame, row = lax.axis_index("wide"), lax.axis_index("narrow")
    part, x = frame // QUAD * 2 + frame % 2, frame // 2 % 2
    scalars = (win_start, text_len, jnp.stack([frame, row, part, x]).astype(jnp.int32))
    firsts = [sum(heads for heads, _ in SLOTS[:slot]) for slot in range(len(SLOTS))]
    swap = [(0, 1), (1, 0)]
    near = [lax.ppermute(block, "wide", core_pairs(count)) for block in (video_k, video_v)]
    remote_q = lax.ppermute(text_q, "narrow", swap)
    pairs = {
        slot: pack(firsts[slot], SLOTS[slot][0], scalars, video_k, video_v)
        for slot in range(AHEAD)
    }
    stats, mixed = text_video(
        count // 2, scalars, text_q, remote_q, video_k, video_v, list(pairs.values())
    )
    own_both, own_mixed = text_own(count // 2, text_len, text_q, text_k, text_v)
    local = [text_k, text_v]
    remote = [lax.ppermute(block, "narrow", swap) for block in local]
    every = lax.all_gather(stats, ("narrow", "wide"))
    half = video_q.shape[1] // HDIM // GH
    out = None
    fars = {}

    def arrive(slot):
        kind = SLOTS[slot][1]
        fars[slot] = [lax.ppermute(pairs[slot], "wide", chip_pairs(count, kind))]
        if kind:
            fars[slot][0] = hold(fars[slot][0], pairs[slot + 1])
            fars[slot].append(lax.ppermute(fars[slot][0], "wide", relay_pairs(count, kind)))

    arrive(0)
    for slot, (heads, kind) in enumerate(SLOTS):
        if slot + 1 < len(SLOTS):
            arrive(slot + 1)
        ahead = slot + AHEAD
        following = (firsts[ahead], SLOTS[ahead][0]) if ahead < len(SLOTS) else None
        gates = []
        if slot == 0:
            gates.append(stats)
        if slot + 1 < len(SLOTS) and SLOTS[slot + 1][1]:
            gates.append(fars[slot + 1][0])
        if slot == len(SLOTS) - 2:
            depth = share.shape[1] // 2
            other = lax.dynamic_slice_in_dim(share, (1 - x) * depth, depth, 1)
            other = lax.ppermute(other, "wide", [(i, i ^ 2) for i in range(count)])
            mine = finish(scalars, both, share, other, own_both, own_mixed, [pairs[slot + 1]])
            whole = lax.all_gather(mine, "wide")
            gates.append(mine)
        out, *pair = video_slot(
            firsts[slot], heads, kind, rows, scalars, video_q, video_k, video_v, near,
            fars[slot], local if firsts[slot] < half else remote, following, gates, out,
        )
        if following:
            pairs[ahead] = pair[0]
        if slot == 2:
            both, share = text_sums(count, stats, mixed, hold(every, pairs[ahead]))
    whole = whole.astype(jnp.bfloat16).reshape(rows, 2, 2, *whole.shape[1:])
    text_out = jnp.transpose(whole, (5, 3, 0, 2, 1, 4)).reshape(TXT, -1)
    return out, text_out


def solution(mesh):
    tokens = P(("wide", "narrow"), None)
    text = P(None, "narrow")
    whole_rows = mesh.shape["narrow"] == GH and mesh.shape["wide"] == 4 * QUAD
    return jax.shard_map(
        keep_rows if whole_rows else split_heads,
        mesh=mesh,
        in_specs=(tokens, tokens, tokens, text, text, text, P(), P()),
        out_specs=(tokens, text),
        check_vma=False,
    )
```

```python
import functools

import jax
import jax.numpy as jnp
from jax import lax
from jax.experimental import pallas as pl
from jax.experimental.pallas import tpu as pltpu
from jax.sharding import PartitionSpec as P

HDIM = 128
TT = 6
TH = 8
TW = 8
GH = 2
GW = 3
KT = 3
KW = 2
TXT = 256


def extended(cells, sides, width):
    for axis, dim in sides:
        count = lax.axis_size(axis)
        ends = count - 1
        head = lax.slice_in_dim(cells, 0, width, axis=dim)
        tail = lax.slice_in_dim(cells, cells.shape[dim] - width, cells.shape[dim], axis=dim)
        cells = jnp.concatenate(
            [
                lax.ppermute(tail, axis, [(i, (i + 1) % count) for i in range(ends)]),
                cells,
                lax.ppermute(head, axis, [((i + 1) % count, i) for i in range(ends)]),
            ],
            axis=dim,
        )
    return cells


def softmax_parts(queries, key_block, value_block, usable, score_scale):
    scores = (
        jnp.einsum("qhd,khd->hqk", queries, key_block, preferred_element_type=jnp.float32)
        * score_scale
    )
    if usable is not None:
        scores = jnp.where(usable[None, None, :], scores, -jnp.inf)
    peak = jnp.max(scores, axis=-1)
    weights = jnp.exp(scores - peak[:, :, None])
    totals = jnp.sum(weights, axis=-1)
    probs = weights.astype(jnp.bfloat16)
    accumulated = jnp.einsum("hqk,khd->qhd", probs, value_block, preferred_element_type=jnp.float32)
    return (peak, totals, accumulated)


def split_heads(video_q, video_k, video_v, text_q, text_k, text_v, text_len, win_start):
    features = text_q.shape[1]
    local_heads = features // HDIM
    slab_count = lax.axis_size("wide")
    position = lax.axis_index("wide")
    slab_rows = video_q.shape[0] * lax.axis_size("narrow")
    tile_rows = TT * TH * TW
    tiles_here = slab_rows // tile_rows
    window_rows = KW * tile_rows
    reach = KT // 2
    score_scale = HDIM ** (-0.5)
    key_value = jnp.stack([video_k, video_v])
    query_set, pair_set = (
        lax.all_to_all(video_q[None], "narrow", split_axis=2, concat_axis=1, tiled=True),
        lax.all_to_all(key_value, "narrow", split_axis=2, concat_axis=1, tiled=True),
    )
    queries_all = query_set[0]
    beside_all = extended(pair_set[:, None], (("wide", 1),), reach)
    stacked = beside_all.reshape(2, KT * slab_rows, features)
    own_slab = beside_all[:, reach]
    text_pair = jnp.stack([text_k, text_v])
    text_usable = jnp.arange(TXT) < text_len[0]
    usable_parts = []
    for depth in range(KT):
        exists = (position + depth - reach >= 0) & (position + depth - reach < slab_count)
        usable_parts.append(jnp.broadcast_to(exists, (window_rows,)))
    usable = jnp.concatenate(usable_parts + [text_usable], 0)
    starts = lax.dynamic_slice_in_dim(win_start, position * tiles_here, tiles_here)

    def one_tile(entry):
        which, first_col = entry
        tile_row = which // GW
        offset = (tile_row * GW + first_col) * tile_rows
        pieces = [
            lax.dynamic_slice_in_dim(stacked, depth * slab_rows + offset, window_rows, 1)
            for depth in range(KT)
        ]
        key_block = jnp.concatenate(pieces + [text_pair], 1).reshape(2, -1, local_heads, HDIM)
        queries = lax.dynamic_slice_in_dim(queries_all, which * tile_rows, tile_rows, 0).reshape(
            tile_rows, local_heads, HDIM
        )
        peak, totals, accumulated = softmax_parts(
            queries, key_block[0], key_block[1], usable, score_scale
        )
        result = accumulated / jnp.transpose(totals)[:, :, None]
        return result.reshape(tile_rows, features).astype(jnp.bfloat16)

    attended = lax.map(one_tile, (jnp.arange(tiles_here, dtype=jnp.int32), starts))
    attended = attended.reshape(slab_rows, features)
    video_out = lax.all_to_all(attended, "narrow", split_axis=0, concat_axis=1, tiled=True)
    text_queries = text_q.reshape(TXT, local_heads, HDIM)
    slab_keys = own_slab[0].reshape(slab_rows, local_heads, HDIM)
    slab_values = own_slab[1].reshape(slab_rows, local_heads, HDIM)
    tile_peak, tile_sum, tile_acc = softmax_parts(
        text_queries, slab_keys, slab_values, None, score_scale
    )
    ceiling = lax.pmax(tile_peak, "wide")
    rescale = jnp.exp(tile_peak - ceiling)
    totals, accumulated = lax.psum(
        (rescale * tile_sum, jnp.transpose(rescale)[:, :, None] * tile_acc), "wide"
    )
    text_keys = text_k.reshape(TXT, local_heads, HDIM)
    text_values = text_v.reshape(TXT, local_heads, HDIM)
    self_peak, self_sum, self_acc = softmax_parts(
        text_queries, text_keys, text_values, text_usable, score_scale
    )
    top = jnp.maximum(ceiling, self_peak)
    video_scale = jnp.exp(ceiling - top)
    self_scale = jnp.exp(self_peak - top)
    numerator = (
        jnp.transpose(video_scale)[:, :, None] * accumulated
        + jnp.transpose(self_scale)[:, :, None] * self_acc
    )
    denominator = video_scale * totals + self_scale * self_sum
    text_out = (
        (numerator / jnp.transpose(denominator)[:, :, None])
        .reshape(TXT, features)
        .astype(jnp.bfloat16)
    )
    return (video_out, text_out)


TILE = TT * TH * TW
WINDOW = KW * TILE
ROW = GW * TILE
EXP2_SCALE = HDIM**-0.5 * 1.4426950408889634
QUAD = 4
SLOTS = (
    (1, 0), (2, 0), (3, 1), (3, 2), (3, 3), (3, 1), (3, 2), (3, 3), (2, 0), (1, 0),
)
AHEAD = 3
SCALE = 2
FINISH = 7
BY_ROWS = (((1,), (1,)), ((), ()))
PLAIN = (((1,), (0,)), ((), ()))
BY_COLS = (((0,), (0,)), ((), ()))
ANY = pl.BlockSpec(memory_space=pl.ANY)


def dot(a, b, dims):
    return lax.dot_general(a, b, dims, preferred_element_type=jnp.float32)


def core_pairs(count):
    return [(i, i ^ 1) for i in range(count)]


def mirrored(count, pairs):
    return pairs + [(count - 1 - a, count - 1 - b) for a, b in pairs]


def chip_pairs(count, kind):
    pairs = [(i, i + 1) for i in range(1, count - 1, QUAD)]
    for z in range(count // QUAD - 1):
        end = QUAD * z + QUAD - 1
        pairs.append((end, QUAD * z if z < kind else end + 1))
    return mirrored(count, pairs)


def relay_pairs(count, kind):
    rows = count // QUAD
    return mirrored(count, [(QUAD * z, QUAD * z + QUAD) for z in range(min(kind, rows - 1))])


def pack_kernel(place, k, v, *rest):
    pair = rest[-1]
    pair[0], pair[1] = k[...], v[...]


def rotated(first, row, heads):
    return (first + row * (heads // GH)) % heads


def pack(first, heads, scalars, k, v, gates):
    every = k.shape[1] // HDIM
    own = pl.BlockSpec((ROW, HDIM), lambda h, place: (0, rotated(first, place[1], every) + h))
    return pl.pallas_call(
        pack_kernel,
        grid_spec=pltpu.PrefetchScalarGridSpec(
            num_scalar_prefetch=1,
            grid=(heads,),
            in_specs=[own, own] + [ANY] * len(gates),
            out_specs=pl.BlockSpec((2, ROW, HDIM), lambda h, _: (0, 0, h)),
        ),
        out_shape=jax.ShapeDtypeStruct((2, ROW, heads * HDIM), k.dtype),
        cost_estimate=pl.CostEstimate(
            flops=0, bytes_accessed=heads * ROW * HDIM * 8, transcendentals=0
        ),
        name="pack_slot",
    )(scalars[-1], k, v, *gates)


def video_kernel(kind, rows, packs, win_start, text_len, place, q, k, v, *rest):
    near_k, near_v, far, text_k, text_v = rest[:5]
    relay = rest[5] if kind else None
    frame, row = place[0], place[1]
    z, at = frame // QUAD, frame % QUAD
    has_far = (frame > 0) & (frame < rows * QUAD - 1)
    relayed = ((at == 0) & (z <= kind)) | ((at == QUAD - 1) & (z >= rows - 1 - kind))
    usable = lax.broadcasted_iota(jnp.int32, (TILE, TXT), 1) < text_len[0]
    if packs:
        next_k, next_v = rest[5 + bool(kind) :][:2]
        pair = rest[-1]
        pair[0], pair[1] = next_k[...], next_v[...]
    out = rest[-2] if packs else rest[-1]

    for tile in range(GW):
        here = pl.ds(tile * TILE, TILE)
        start = win_start[(frame * GH + row) * GW + tile]
        window = pl.ds(pl.multiple_of(start * TILE, TILE), WINDOW)
        own = k[window, :]
        far_k, far_v = far[0, window, :], far[1, window, :]
        if kind:
            far_k = jnp.where(relayed, relay[0, window, :], far_k)
            far_v = jnp.where(relayed, relay[1, window, :], far_v)
        keys = [text_k[...], own, near_k[window, :], jnp.where(has_far, far_k, own)]
        values = [text_v[...], v[window, :], near_v[window, :], far_v]
        queries = q[here, :]
        scores = [dot(queries, block, BY_ROWS) for block in keys]
        scores[0] = jnp.where(usable, scores[0], -jnp.inf)
        peak = functools.reduce(
            jnp.maximum, [jnp.max(block, axis=1, keepdims=True) for block in scores]
        )
        mixed = jnp.zeros((TILE, HDIM), jnp.float32)
        sums = []
        for block, value in zip(scores, values):
            weights = jnp.exp2((block - peak) * EXP2_SCALE)
            sums.append(jnp.sum(weights, axis=1, keepdims=True))
            mixed += dot(weights.astype(jnp.bfloat16), value, PLAIN)
        total = sums[0] + sums[1] + sums[2] + jnp.where(has_far, sums[3], 0.0)
        out[here, :] = (mixed / total).astype(jnp.bfloat16)


def video_slot(first, heads, kind, rows, scalars, q, k, v, near, far, text, following, gates, out):
    every = q.shape[1] // HDIM

    def columns(first, per, last):
        return pl.BlockSpec(
            (ROW, per * HDIM),
            lambda h, *s: (0, rotated(first, s[2][1], every) // per + jnp.minimum(h, last)),
        )

    own = columns(first, 1, heads - 1)
    halo = pl.BlockSpec((2, ROW, HDIM), lambda h, *_: (0, 0, h))
    prompt = pl.BlockSpec((TXT, HDIM), lambda h, *_: (0, first % (every // GH) + h))
    keys = KT * WINDOW + TXT
    inputs = [q, k, v, *near, far[0], *text]
    specs = [own] * 5 + [halo, prompt, prompt]
    if kind:
        inputs, specs = inputs + [far[1]], specs + [halo]
    out_specs = [own]
    out_shape = [jax.ShapeDtypeStruct(q.shape, q.dtype)]
    if following:
        next_first, next_heads = following
        per = 1 if next_heads <= heads else next_heads
        last = next_heads // per - 1
        inputs = inputs + [k, v]
        specs = specs + [columns(next_first, per, last)] * 2
        out_specs.append(
            pl.BlockSpec((2, ROW, per * HDIM), lambda h, *_: (0, 0, jnp.minimum(h, last)))
        )
        out_shape.append(jax.ShapeDtypeStruct((2, ROW, next_heads * HDIM), k.dtype))
    inputs, specs = inputs + list(gates), specs + [ANY] * len(gates)
    aliases = {}
    if out is not None:
        inputs, specs = inputs + [out], specs + [ANY]
        aliases = {len(scalars) + len(inputs) - 1: 0}
    return pl.pallas_call(
        functools.partial(video_kernel, kind, rows, bool(following)),
        grid_spec=pltpu.PrefetchScalarGridSpec(
            num_scalar_prefetch=len(scalars),
            grid=(heads,),
            in_specs=specs,
            out_specs=out_specs,
        ),
        out_shape=out_shape,
        input_output_aliases=aliases,
        compiler_params=pltpu.CompilerParams(vmem_limit_bytes=48 * 2**20),
        cost_estimate=pl.CostEstimate(
            flops=heads * ROW * keys * HDIM * 4,
            bytes_accessed=heads * ROW * HDIM * 16,
            transcendentals=heads * ROW * keys,
        ),
        name="video_attention",
    )(*scalars, *inputs)


def text_sums_kernel(text_q, k, v, usable, stats, mixed):
    scores = dot(k, text_q, BY_ROWS)
    if usable is not None:
        scores = jnp.where(usable, scores, -jnp.inf)
    top = jnp.max(scores, axis=0, keepdims=True)
    weights = jnp.exp2((scores - top) * EXP2_SCALE)
    stats[0, 0:1], stats[0, 1:2] = top, jnp.sum(weights, axis=0, keepdims=True)
    sums = dot(v, weights.astype(jnp.bfloat16), BY_COLS)
    mixed[:, 0] = sums.reshape(mixed.shape[0], HDIM // mixed.shape[0], TXT)


def text_video_kernel(half, place, local_q, remote_q, k, v, *rest):
    queries = jnp.where(pl.program_id(0) < half, local_q[...], remote_q[...])
    text_sums_kernel(queries, k[...], v[...], None, *rest[-2:])


def text_own_kernel(text_len, text_q, text_k, text_v, stats, mixed):
    usable = lax.broadcasted_iota(jnp.int32, (TXT, TXT), 0) < text_len[0]
    text_sums_kernel(text_q[...], text_k[...], text_v[...], usable, stats, mixed)


def text_video(shares, scalars, local_q, remote_q, k, v, gates):
    heads = k.shape[1] // HDIM
    half = heads // GH
    depth = HDIM // shares

    def head(h, place):
        return (h + place[1] * half) % heads

    own = pl.BlockSpec((ROW, HDIM), lambda h, place: (0, head(h, place)))
    return pl.pallas_call(
        functools.partial(text_video_kernel, half),
        grid_spec=pltpu.PrefetchScalarGridSpec(
            num_scalar_prefetch=1,
            grid=(heads,),
            in_specs=[
                pl.BlockSpec((TXT, HDIM), lambda h, _: (0, jnp.minimum(h, half - 1))),
                pl.BlockSpec((TXT, HDIM), lambda h, _: (0, jnp.maximum(h - half, 0))),
                own,
                own,
            ]
            + [ANY] * len(gates),
            out_specs=[
                pl.BlockSpec((1, 2, TXT), lambda h, place: (head(h, place), 0, 0)),
                pl.BlockSpec(
                    (shares, 1, depth, TXT),
                    lambda h, place: (head(h, place) // half, h % half, 0, 0),
                ),
            ],
        ),
        out_shape=[
            jax.ShapeDtypeStruct((heads, 2, TXT), jnp.float32),
            jax.ShapeDtypeStruct((GH * shares, half, depth, TXT), jnp.float32),
        ],
        compiler_params=pltpu.CompilerParams(vmem_limit_bytes=48 * 2**20),
        cost_estimate=pl.CostEstimate(
            flops=heads * ROW * TXT * HDIM * 4,
            bytes_accessed=heads * (ROW + TXT) * HDIM * 4,
            transcendentals=heads * ROW * TXT,
        ),
        name="text_over_video",
    )(scalars[-1], local_q, remote_q, k, v, *gates)


def text_own(shares, text_len, text_q, text_k, text_v):
    heads = text_q.shape[1] // HDIM
    depth = HDIM // shares
    text = pl.BlockSpec((TXT, HDIM), lambda h, _: (0, h))
    return pl.pallas_call(
        text_own_kernel,
        grid_spec=pltpu.PrefetchScalarGridSpec(
            num_scalar_prefetch=1,
            grid=(heads,),
            in_specs=[text] * 3,
            out_specs=[
                pl.BlockSpec((1, 2, TXT), lambda h, _: (h, 0, 0)),
                pl.BlockSpec((shares, 1, depth, TXT), lambda h, _: (0, h, 0, 0)),
            ],
        ),
        out_shape=[
            jax.ShapeDtypeStruct((heads, 2, TXT), jnp.float32),
            jax.ShapeDtypeStruct((shares, heads, depth, TXT), jnp.float32),
        ],
        cost_estimate=pl.CostEstimate(
            flops=heads * TXT * TXT * HDIM * 4,
            bytes_accessed=heads * TXT * HDIM * 10,
            transcendentals=heads * TXT * TXT,
        ),
        name="text_over_text",
    )(text_len, text_q, text_k, text_v)


def finish_kernel(place, both, share, other, own_both, own_share, *rest):
    def parts(ref):
        return ref[:, 0:1, :], ref[:, 1:2, :]

    top, total = parts(both)
    own_top, own_total = parts(own_both)
    peak = jnp.maximum(top, own_top)
    scale = jnp.exp2((top - peak) * EXP2_SCALE)
    own_scale = jnp.exp2((own_top - peak) * EXP2_SCALE)
    mixed = scale * (share[...] + other[...]) + own_scale * own_share[0]
    rest[-1][...] = (mixed / (scale * total + own_scale * own_total)).astype(jnp.bfloat16)


def finish(scalars, both, share, other, own_both, own_mixed, gates):
    half, depth, queries = other.shape
    local = pl.BlockSpec((half, depth, queries), lambda i, *_: (0, 0, 0))
    return pl.pallas_call(
        finish_kernel,
        grid_spec=pltpu.PrefetchScalarGridSpec(
            num_scalar_prefetch=1,
            grid=(1,),
            in_specs=[
                pl.BlockSpec((half, 2, queries), lambda i, place: (place[1], 0, 0)),
                pl.BlockSpec((half, depth, queries), lambda i, place: (0, place[3], 0)),
                local,
                pl.BlockSpec((half, 2, queries), lambda i, *_: (0, 0, 0)),
                pl.BlockSpec(
                    (1, half, depth, queries), lambda i, place: (place[2], 0, place[3], 0)
                ),
            ]
            + [ANY] * len(gates),
            out_specs=local,
        ),
        out_shape=jax.ShapeDtypeStruct(other.shape, jnp.bfloat16),
        name="finish_text",
    )(scalars[-1], both, share, other, own_both, own_mixed, *gates)


def text_sums(count, stats, mixed, every):
    shares = count // 2
    half = mixed.shape[1]
    groups = [[n * count + i for n in range(GH) for i in column] for column in columns(count)]
    peaks, totals = every[:, :, 0], every[:, :, 1]
    top = jnp.max(peaks, axis=0)
    total = jnp.sum(jnp.exp2((peaks - top) * EXP2_SCALE) * totals, axis=0)
    scale = jnp.exp2((stats[:, 0] - top) * EXP2_SCALE).reshape(GH, 1, half, 1, TXT)
    scaled = scale * mixed.reshape(GH, shares, half, -1, TXT)
    share = lax.psum_scatter(
        scaled.reshape(mixed.shape),
        ("narrow", "wide"),
        scatter_dimension=0,
        axis_index_groups=groups,
    )
    return jnp.stack([top, total], 1), share


def columns(count):
    return [[i for i in range(count) if i % QUAD // 2 == x] for x in range(2)]


def hold_kernel(block, gate, out):
    pass


def hold(block, gate):
    return pl.pallas_call(
        hold_kernel,
        in_specs=[ANY, ANY],
        out_specs=ANY,
        out_shape=jax.ShapeDtypeStruct(block.shape, block.dtype),
        input_output_aliases={0: 0},
        name="hold_slot",
    )(block, gate)


def keep_rows(video_q, video_k, video_v, text_q, text_k, text_v, text_len, win_start):
    count = lax.axis_size("wide")
    rows = count // QUAD
    frame, row = lax.axis_index("wide"), lax.axis_index("narrow")
    part, x = frame // QUAD * 2 + frame % 2, frame // 2 % 2
    scalars = (win_start, text_len, jnp.stack([frame, row, part, x]).astype(jnp.int32))
    firsts = [sum(heads for heads, _ in SLOTS[:slot]) for slot in range(len(SLOTS))]
    swap = [(0, 1), (1, 0)]
    near = [lax.ppermute(block, "wide", core_pairs(count)) for block in (video_k, video_v)]
    remote_q = lax.ppermute(text_q, "narrow", swap)
    pairs = {}
    for slot in range(AHEAD):
        gates = [pairs[slot - 1]] if slot else []
        pairs[slot] = pack(firsts[slot], SLOTS[slot][0], scalars, video_k, video_v, gates)
    fars = {
        slot: [lax.ppermute(pairs[slot], "wide", chip_pairs(count, SLOTS[slot][1]))]
        for slot in range(2)
    }
    stats, mixed = text_video(
        count // 2, scalars, text_q, remote_q, video_k, video_v, [pairs[AHEAD - 1], fars[0][0], fars[1][0]]
    )
    own_both, own_mixed = text_own(count // 2, text_len, text_q, text_k, text_v)
    local = [text_k, text_v]
    remote = [lax.ppermute(block, "narrow", swap) for block in local]
    every = lax.all_gather(stats, ("narrow", "wide"))
    half = video_q.shape[1] // HDIM // GH
    out = None

    def arrive(slot):
        kind = SLOTS[slot][1]
        fars[slot] = [lax.ppermute(pairs[slot], "wide", chip_pairs(count, kind))]
        if kind:
            fars[slot][0] = hold(fars[slot][0], pairs[slot + 1])
            fars[slot].append(lax.ppermute(fars[slot][0], "wide", relay_pairs(count, kind)))

    for slot, (heads, kind) in enumerate(SLOTS):
        if 1 < slot + 1 < len(SLOTS):
            arrive(slot + 1)
        ahead = slot + AHEAD
        following = (firsts[ahead], SLOTS[ahead][0]) if ahead < len(SLOTS) else None
        gates = []
        if slot == 1:
            gates.append(stats)
        if slot + 1 < len(SLOTS) and SLOTS[slot + 1][1]:
            gates.append(fars[slot + 1][0])
        if slot == FINISH:
            depth = share.shape[1] // 2
            other = lax.dynamic_slice_in_dim(share, (1 - x) * depth, depth, 1)
            other = lax.ppermute(other, "wide", [(i, i ^ 2) for i in range(count)])
            mine = finish(scalars, both, share, other, own_both, own_mixed, [pairs[slot + 1]])
            whole = lax.all_gather(mine, ("narrow", "wide"))
            gates.append(mine)
        out, *pair = video_slot(
            firsts[slot], heads, kind, rows, scalars, video_q, video_k, video_v, near,
            fars[slot], local if firsts[slot] < half else remote, following, gates, out,
        )
        if following:
            pairs[ahead] = pair[0]
        if slot == SCALE:
            both, share = text_sums(count, stats, mixed, hold(every, pairs[ahead]))
    whole = lax.dynamic_slice_in_dim(whole, row * count, count)
    whole = whole.reshape(rows, 2, 2, *whole.shape[1:])
    text_out = jnp.transpose(whole, (5, 3, 0, 2, 1, 4)).reshape(TXT, -1)
    return out, text_out


def solution(mesh):
    tokens = P(("wide", "narrow"), None)
    text = P(None, "narrow")
    whole_rows = mesh.shape["narrow"] == GH and mesh.shape["wide"] == 4 * QUAD
    return jax.shard_map(
        keep_rows if whole_rows else split_heads,
        mesh=mesh,
        in_specs=(tokens, tokens, tokens, text, text, text, P(), P()),
        out_specs=(tokens, text),
        check_vma=False,
    )
```
